256 devices in a mesh: section: 2 (over core), grp: 4 (over y), ctx: 32 (over x, z).
Axes of the slice: x: 4, y: 4, z: 8, core: 2. Of those that a mesh axis runs over, the one named last changes fastest.
Arguments:
- q_pf: bfloat16 [2, 4, 4096, 4096], P('section', 'grp', 'ctx'), may hold values from -16 to 16
- k_pf: bfloat16 [2, 4, 4096, 1024], P('section', 'grp', 'ctx'), may hold values from -16 to 16
- v_pf: bfloat16 [2, 4, 4096, 1024], P('section', 'grp', 'ctx'), may hold values from -6 to 6
- pf_blocks: int32 [2, 4, 2], P(None, 'grp'), may hold values from 1 to 192, 256 in all within a row
- slot_order: int32 [2, 4, 16], P(None, 'grp'), may hold values from 0 to 15, each once within a row
- cache_k: bfloat16 [2, 4, 128, 4096, 128], P('section', 'grp', 'ctx'), may hold values from -6 to 6
- cache_v: bfloat16 [2, 4, 128, 4096, 128], P('section', 'grp', 'ctx'), may hold values from -6 to 6
- ctx_len: int32 [2, 4, 16], P('section', 'grp'), may hold values from 1 to 4096
- q_dec: bfloat16 [2, 4, 128, 4, 512], P('section', 'grp', 'ctx'), may hold values from -16 to 16
- k_new: bfloat16 [2, 4, 128, 4, 128], P('section', 'grp', 'ctx'), may hold values from -16 to 16
- v_new: bfloat16 [2, 4, 128, 4, 128], P('section', 'grp', 'ctx'), may hold values from -6 to 6
Outputs:
- pf_out: bfloat16 [2, 4, 4096, 4096], P('section', 'grp', 'ctx')
- dec_out: bfloat16 [2, 4, 128, 4, 512], P('section', 'grp', 'ctx')
The draws below stay inside these ranges and needn't reach their ends.
Inputs may be any that keep to these rules, and one draw needn't show every extreme that they name: `pf_blocks`: the 2 counts of a row sum to 256.
All inputs are finite; a program needn't handle non-finite values.
Results may differ from the reference program's by a relative error of at most 0.0055.
Values may be sent and summed in bfloat16 or wider, within the bound.
No kernel may reach another device: no remote copies, remote signals or barrier semaphores. Data moves between devices by JAX's collectives and lax.ppermute only.
A program may use at most 128 MiB of HBM per device.

```python
import math
import jax
import jax.numpy as jnp
import numpy as np
from jax import lax

HD = 128
KVH = 8
QH = 32
RATIO = 4
BLOCK = 16
CTX = 4096
REQS_G = 16
PF_REQS = 2
STEPS = 4
POOLS = 2
GROUPS = 4
TOKENS = 4096
SLOTS = 128


def draw_q_pf(key, part):
    key = jax.random.fold_in(key, 11)
    layout = (POOLS, GROUPS, TOKENS, KVH, RATIO, HD)
    drawn = jnp.clip(jax.random.normal(key, layout, jnp.float32), -6.0, 6.0)
    return drawn.reshape(POOLS, GROUPS, TOKENS, QH * HD).astype(jnp.bfloat16)


def draw_k_pf(key, part):
    key = jax.random.fold_in(key, 12)
    layout = (POOLS, GROUPS, TOKENS, KVH, HD)
    drawn = jnp.clip(jax.random.normal(key, layout, jnp.float32), -6.0, 6.0)
    return drawn.reshape(POOLS, GROUPS, TOKENS, KVH * HD).astype(jnp.bfloat16)


def draw_q_dec(key, part):
    key = jax.random.fold_in(key, 13)
    layout = (POOLS, GROUPS, SLOTS, STEPS, RATIO, HD)
    drawn = jnp.clip(jax.random.normal(key, layout, jnp.float32), -6.0, 6.0)
    return drawn.reshape(POOLS, GROUPS, SLOTS, STEPS, RATIO * HD).astype(jnp.bfloat16)


def draw_k_new(key, part):
    key = jax.random.fold_in(key, 14)
    layout = (POOLS, GROUPS, SLOTS, STEPS, HD)
    drawn = jnp.clip(jax.random.normal(key, layout, jnp.float32), -6.0, 6.0)
    return drawn.astype(jnp.bfloat16)


def touch_ends(array, own_key, smallest, top_value):
    longest = array.shape.index(max(array.shape))
    spots = []
    for shift in (0, 1):
        where = [jax.random.randint(jax.random.fold_in(own_key, axis), (), 0, length) for axis, length in enumerate(array.shape)]
        where[longest] = (where[longest] + shift) % array.shape[longest]
        spots.append(tuple(where))
    return array.at[spots[0]].set(smallest).at[spots[1]].set(top_value)


def shard_levels(key, dims, cuts, low, top_value):
    level = 1.0
    for position, shards_of in cuts:
        steps = jax.random.uniform(jax.random.fold_in(jax.random.fold_in(key, 6), position), (shards_of,), jnp.float32, low / len(cuts), top_value / len(cuts))
        level = level * jnp.repeat(jnp.exp(steps), dims[position] // shards_of).reshape((-1,) + (1,) * (len(dims) - 1 - position))
    return level


def split_up(number_of, total, bound, lean):
    portions = [(1 << 20) // math.isqrt(standing ** lean) + 1 for standing in range(2, number_of + 1)]
    spare, holding = total - bound - (number_of - 1), [1] * (number_of - 1)
    while spare > 0:
        candidates = [i for i in range(number_of - 1) if holding[i] < bound]
        whole, budget = sum([portions[i] for i in candidates]), spare
        for i in candidates:
            more = min(bound - holding[i], max(1, budget * portions[i] // whole), spare)
            holding[i] = holding[i] + more
            spare = spare - more
    return np.array([bound] + holding)


def uneven(rng, number_of, total, limit, slope):
    if number_of == 2:
        one = jax.random.randint(rng, (), max(1, total - limit), min(limit, total - 1) + 1)
        return jnp.stack([one, total - one])
    sizes = jnp.asarray(split_up(number_of, total, limit, slope), jnp.int32)
    twos = (number_of - 1) // 2
    source_of, sink = sizes[1:1 + 2 * twos:2], sizes[2:2 + 2 * twos:2]
    room = jnp.minimum(source_of - 1, limit - sink)
    passed = jax.random.randint(jax.random.fold_in(rng, 1), (twos,), 0, 1 << 20) % (room + 1)
    sizes = sizes.at[1:1 + 2 * twos:2].set(source_of - passed).at[2:2 + 2 * twos:2].set(sink + passed)
    return sizes[jax.random.permutation(jax.random.fold_in(rng, 2), number_of)]


def bell_draw(own_key, extent, deviation, reach, cuts=(), kind=jnp.bfloat16):
    values = jax.random.normal(own_key, extent, jnp.float32) * deviation
    if len(cuts) > 0:
        values = shard_levels(own_key, extent, cuts, -0.22, 0.18) * values
    return jnp.clip(values, min=-reach, max=reach).astype(kind)


def setup_inputs(seed: int = 0) -> dict:
    key_list = jax.random.split(jax.random.key(seed), 12)
    return {
        "q_pf": draw_q_pf(jax.random.fold_in(key_list[11], 71), 0),
        "k_pf": draw_k_pf(jax.random.fold_in(key_list[11], 71), 0),
        "v_pf": bell_draw(key_list[2], (POOLS, GROUPS, TOKENS, KVH * HD), 1.0, 6.0, ((0, 2), (1, 4), (2, 32))),
        "pf_blocks": jax.vmap(lambda own: uneven(own, PF_REQS, TOKENS // BLOCK, min(CTX // BLOCK, 3 * TOKENS // BLOCK // 4), 2))(jax.random.split(key_list[3], POOLS * GROUPS)).reshape((POOLS, GROUPS, PF_REQS)).astype(jnp.int32),
        "slot_order": jax.vmap(lambda own: jax.random.permutation(own, REQS_G))(jax.random.split(key_list[4], POOLS * GROUPS)).reshape((POOLS, GROUPS, REQS_G)).astype(jnp.int32),
        "cache_k": bell_draw(key_list[5], (POOLS, GROUPS, SLOTS, CTX, HD), 1.0, 6.0, ((0, 2), (1, 4), (2, 32))),
        "cache_v": bell_draw(key_list[6], (POOLS, GROUPS, SLOTS, CTX, HD), 1.0, 6.0, ((0, 2), (1, 4), (2, 32))),
        "ctx_len": touch_ends(jax.random.randint(key_list[7], (POOLS, GROUPS, REQS_G), 1, CTX + 1), jax.random.fold_in(key_list[7], 1), 1, CTX).astype(jnp.int32),
        "q_dec": draw_q_dec(jax.random.fold_in(key_list[11], 71), 0),
        "k_new": draw_k_new(jax.random.fold_in(key_list[11], 71), 0),
        "v_new": bell_draw(key_list[10], (POOLS, GROUPS, SLOTS, STEPS, HD), 1.0, 6.0, ((0, 2), (1, 4), (2, 32))),
    }


masked_score = -1e+30

def span_layout(block_counts):
    req_lengths = (block_counts * BLOCK).astype(jnp.int32)
    req_ends = jnp.cumsum(req_lengths).astype(jnp.int32)
    req_starts = req_ends - req_lengths
    positions = jnp.arange(TOKENS, dtype=jnp.int32)
    owners = lax.optimization_barrier(jnp.sum((positions[:, None] >= req_ends[None, :]).astype(jnp.int32), axis=1))
    return (req_lengths, req_starts, owners)

def prefill_head(queries, key_rows, value_rows, owners):
    inv_root = 1.0 / math.sqrt(HD)
    block_rows = math.gcd(TOKENS, 512)
    positions = jnp.arange(TOKENS, dtype=jnp.int32)
    keys_wide = key_rows.astype(jnp.float32)
    values_wide = value_rows.astype(jnp.float32)

    def one_block(block_index):
        first_row = block_index * block_rows
        block_q = lax.dynamic_slice_in_dim(queries, first_row, block_rows, 0).astype(jnp.float32)
        block_pos = first_row + jnp.arange(block_rows, dtype=jnp.int32)
        block_owner = lax.dynamic_slice_in_dim(owners, first_row, block_rows, 0)
        allowed = (owners[None, :] == block_owner[:, None]) & (positions[None, :] <= block_pos[:, None])
        scores = jnp.einsum('qrd,kd->rqk', block_q, keys_wide) * inv_root
        scores = jnp.where(allowed[None], scores, masked_score)
        row_max = lax.optimization_barrier(jnp.max(scores, axis=-1, keepdims=True))
        weights = jnp.where(allowed[None], jnp.exp(scores - row_max), 0.0)
        row_sum = lax.optimization_barrier(jnp.sum(weights, axis=-1))
        rounded = lax.optimization_barrier(weights.astype(jnp.bfloat16)).astype(jnp.float32)
        weighted = jnp.einsum('rqk,kd->qrd', rounded, values_wide)
        return (weighted / jnp.transpose(row_sum)[:, :, None]).astype(jnp.bfloat16)
    blocks = lax.map(one_block, jnp.arange(TOKENS // block_rows, dtype=jnp.int32))
    return blocks.reshape(TOKENS, RATIO, HD)

def prefill_group(q_rows, k_rows, v_rows, block_counts):
    req_lengths, req_starts, owners = span_layout(block_counts)
    queries = q_rows.reshape(TOKENS, KVH, RATIO, HD).transpose(1, 0, 2, 3)
    key_heads = k_rows.reshape(TOKENS, KVH, HD).transpose(1, 0, 2)
    value_heads = v_rows.reshape(TOKENS, KVH, HD).transpose(1, 0, 2)

    def one_head(head_parts):
        return prefill_head(head_parts[0], head_parts[1], head_parts[2], owners)
    outputs = lax.map(one_head, (queries, key_heads, value_heads))
    return outputs.transpose(1, 0, 2, 3).reshape(TOKENS, QH * HD)

def decode_rows(query_rows, keys_full, values_full, fresh_keys, fresh_values, live_len):
    row_count = query_rows.shape[0]
    queries = query_rows.reshape(row_count, STEPS, RATIO, HD).astype(jnp.float32)
    inv_root = 1.0 / math.sqrt(HD)
    cache_ok = (jnp.arange(CTX, dtype=jnp.int32)[None, :] < live_len[:, None])[:, None, None, :]
    step_ids = jnp.arange(STEPS, dtype=jnp.int32)
    fresh_ok = (step_ids[None, :] <= step_ids[:, None])[None, :, None, :]
    cache_scores = jnp.einsum('ntrd,ncd->ntrc', queries, keys_full.astype(jnp.float32)) * inv_root
    cache_scores = jnp.where(cache_ok, cache_scores, masked_score)
    fresh_scores = jnp.einsum('ntrd,nud->ntru', queries, fresh_keys.astype(jnp.float32)) * inv_root
    fresh_scores = jnp.where(fresh_ok, fresh_scores, masked_score)
    row_max = jnp.maximum(lax.optimization_barrier(jnp.max(cache_scores, axis=-1)), lax.optimization_barrier(jnp.max(fresh_scores, axis=-1)))[..., None]
    cache_w = jnp.where(cache_ok, jnp.exp(cache_scores - row_max), 0.0)
    fresh_w = jnp.where(fresh_ok, jnp.exp(fresh_scores - row_max), 0.0)
    row_sum = lax.optimization_barrier(jnp.sum(cache_w, axis=-1)) + lax.optimization_barrier(jnp.sum(fresh_w, axis=-1))
    cache_round = lax.optimization_barrier(cache_w.astype(jnp.bfloat16)).astype(jnp.float32)
    fresh_round = lax.optimization_barrier(fresh_w.astype(jnp.bfloat16)).astype(jnp.float32)
    weighted = jnp.einsum('ntrc,ncd->ntrd', cache_round, values_full.astype(jnp.float32))
    weighted = weighted + jnp.einsum('ntru,nud->ntrd', fresh_round, fresh_values.astype(jnp.float32))
    return (weighted / row_sum[..., None]).astype(jnp.bfloat16).reshape(row_count, STEPS, RATIO * HD)

def decode_group(span_keys, span_values, block_counts, slot_list, old_lengths, cache_keys, cache_values, q_rows, fresh_keys, fresh_values):
    req_lengths, req_starts, ignored = span_layout(block_counts)
    slot_ids = jnp.arange(REQS_G, dtype=jnp.int32)
    matches = (slot_list[None, :PF_REQS] == slot_ids[:, None]).astype(jnp.int32)
    is_new = lax.optimization_barrier(jnp.sum(matches, axis=1)) > 0
    new_start = lax.optimization_barrier(jnp.sum(matches * req_starts[None, :], axis=1)).astype(jnp.int32)
    new_length = lax.optimization_barrier(jnp.sum(matches * req_lengths[None, :], axis=1)).astype(jnp.int32)
    live_len = jnp.where(is_new, new_length, old_lengths)
    cache_pos = jnp.arange(CTX, dtype=jnp.int32)
    source = jnp.clip(new_start[:, None] + cache_pos[None, :], 0, TOKENS - 1).astype(jnp.int32)
    use_new = is_new[:, None] & (cache_pos[None, :] < new_length[:, None])
    key_heads = span_keys.reshape(TOKENS, KVH, HD).transpose(1, 0, 2)
    value_heads = span_values.reshape(TOKENS, KVH, HD).transpose(1, 0, 2)

    def one_head(head_parts):
        span_k, span_v, cache_kh, cache_vh, query_h, fresh_kh, fresh_vh = head_parts
        keys_full = jnp.where(use_new[:, :, None], span_k[source], cache_kh)
        values_full = jnp.where(use_new[:, :, None], span_v[source], cache_vh)
        return decode_rows(query_h, keys_full, values_full, fresh_kh, fresh_vh, live_len)
    stacked = lax.map(one_head, (key_heads, value_heads, cache_keys.reshape(KVH, REQS_G, CTX, HD), cache_values.reshape(KVH, REQS_G, CTX, HD), q_rows.reshape(KVH, REQS_G, STEPS, RATIO * HD), fresh_keys.reshape(KVH, REQS_G, STEPS, HD), fresh_values.reshape(KVH, REQS_G, STEPS, HD)))
    return stacked.reshape(SLOTS, STEPS, RATIO * HD)

def reference(q_pf, k_pf, v_pf, pf_blocks, slot_order, cache_k, cache_v, ctx_len, q_dec, k_new, v_new):
    prefill_all = []
    decode_all = []
    for pool_index in range(POOLS):
        other_pool = 1 - pool_index
        prefill_row = []
        decode_row = []
        for group_index in range(GROUPS):
            prefill_row.append(prefill_group(q_pf[pool_index, group_index], k_pf[pool_index, group_index], v_pf[pool_index, group_index], pf_blocks[pool_index, group_index]))
            decode_row.append(decode_group(k_pf[other_pool, group_index], v_pf[other_pool, group_index], pf_blocks[other_pool, group_index], slot_order[other_pool, group_index], ctx_len[pool_index, group_index], cache_k[pool_index, group_index], cache_v[pool_index, group_index], q_dec[pool_index, group_index], k_new[pool_index, group_index], v_new[pool_index, group_index]))
        prefill_all.append(jnp.stack(prefill_row))
        decode_all.append(jnp.stack(decode_row))
    return (jnp.stack(prefill_all), jnp.stack(decode_all))
```

```python
import functools
import math

import jax
import jax.numpy as jnp
from jax import lax
from jax.experimental import pallas as pl
from jax.experimental.pallas import tpu as pltpu
from jax.sharding import PartitionSpec as P

HD = 128
BLOCK = 16
NX, NZ = 4, 8
ROWS = 128
XROWS = NZ * ROWS
HEADS = 2
RATIO = 4
STEPS = 4
SLOTS = 16
NEW = 4
MASKED = -1e30
SCALE = math.log2(math.e) / math.sqrt(HD)

ALONG_Z = [[x * NZ + z for z in range(NZ)] for x in range(NX)]
ALONG_X = [[x * NZ + z for x in range(NX)] for z in range(NZ)]

GRANT = 20 << 20

I_SECTION, I_CTX, I_BLOCKS, I_ORDER, I_LEN = 0, 1, 2, 6, 38


def nt(a, b):
    return lax.dot_general(a, b, (((1,), (1,)), ((), ())), preferred_element_type=jnp.float32)


def nn(a, b):
    return lax.dot_general(a, b, (((1,), (0,)), ((), ())), preferred_element_type=jnp.float32)


SAFE = 1e30


def stage_kernel(offsets, start, last, ints, q_ref, *refs):
    n = len(offsets)
    z = ints[I_CTX] % NZ
    first = ints[I_BLOCKS + 2 * ints[I_SECTION]] * BLOCK
    sources = [(z + d) % NZ for d in offsets]
    lanes = [slice(g * HD, (g + 1) * HD) for g in range(n)]
    heads = [slice(a * ROWS, (a + 1) * ROWS) for a in range(RATIO)]
    *refs, m_ref, l_ref = refs
    if start:
        *kvs, rows_out, acc_out = refs
    elif not last:
        *kvs, rows_in, acc_in, rows_out, acc_out = refs
    else:
        *kvs, low_half, high_half, rows_in, acc_in, out_ref, acc_end = refs

    def keys_values(h, c):
        def one(kv, at):
            return kv[pl.ds(at, 1), h].reshape(ROWS, 2 * HD)

        blocks = [one(kv, c) for kv in kvs]
        if last:
            half = NX // 2
            blocks.append(jnp.where(c < half, *[one(kv, c % half) for kv in (low_half, high_half)]))
        k = jnp.concatenate([b[:, :HD] for b in blocks], axis=0)
        v = jnp.concatenate([b[:, HD:] for b in blocks], axis=0)
        return k, v

    def block(x, carry):
        row0 = x * XROWS + z * ROWS
        low = jnp.where(row0 >= first, first // XROWS, 0)
        qx = q_ref[pl.ds(x, 1)].reshape(ROWS, HEADS * RATIO * HD)
        at = [slice(a * HD, (a + 1) * HD) for a in range(HEADS * RATIO)]
        qs = [
            jnp.concatenate([qx[:, at[h * RATIO + a]] for a in range(RATIO)], axis=0)
            for h in range(HEADS)
        ]
        spots = [h * NX + x for h in range(HEADS)]
        ms = [m_ref.at[h] for h in range(HEADS)]
        ls = [l_ref.at[h] for h in range(HEADS)]
        accs = [acc_end.at[h] if last else acc_out.at[spots[h]] for h in range(HEADS)]

        def allowed(c):
            row = row0 + lax.broadcasted_iota(jnp.int32, (ROWS, HD), 0)
            lane = c * XROWS + lax.broadcasted_iota(jnp.int32, (ROWS, HD), 1)
            begin = jnp.where(row < first, 0, first)
            return [(lane + src * ROWS <= row) & (lane + src * ROWS >= begin) for src in sources]

        def careful(c, held):
            ok = allowed(c)
            for h in range(HEADS):
                k, v = keys_values(h, c)
                s = nt(qs[h], k)
                ps = []
                for rs in heads:
                    cols = [jnp.where(o, s[rs, g], MASKED) for g, o in zip(lanes, ok)]
                    top = jnp.max(functools.reduce(jnp.maximum, cols), axis=-1, keepdims=True)
                    old = ms[h][rs] if held else None
                    new = jnp.maximum(old, top) if held else jnp.broadcast_to(top, (ROWS, HD))
                    pg = [jnp.exp2((t - new) * SCALE) for t in cols]
                    ms[h][rs] = new
                    total = functools.reduce(jnp.add, pg)
                    if held:
                        fix = jnp.exp2((old - new) * SCALE)
                        ls[h][rs] = ls[h][rs] * fix + total
                        accs[h][rs] = accs[h][rs] * fix
                    else:
                        ls[h][rs] = total
                    ps.append(jnp.concatenate([t.astype(jnp.bfloat16) for t in pg], axis=1))
                o = nn(jnp.concatenate(ps, axis=0), v)
                accs[h][...] = accs[h][...] + o if held else o

        def quick(c, masked):
            ok = allowed(c) if masked else None
            kvh = [keys_values(h, c) for h in range(HEADS)]
            scores = [nt(qs[h], kvh[h][0]) for h in range(HEADS)]
            for h in range(HEADS):
                s = scores[h]
                ps = []
                for rs in heads:
                    m = ms[h][rs]
                    pg = [jnp.exp2((s[rs, g] - m) * SCALE) for g in lanes]
                    if masked:
                        pg = [jnp.where(o, t, 0.0) for o, t in zip(ok, pg)]
                    ls[h][rs] += functools.reduce(jnp.add, pg)
                    ps.append(jnp.concatenate([t.astype(jnp.bfloat16) for t in pg], axis=1))
                accs[h][...] += nn(jnp.concatenate(ps, axis=0), kvh[h][1])

        def begin():
            if start:
                careful(x, False)
                return
            for h in range(HEADS):
                accs[h][...] = acc_in[pl.ds(spots[h], 1)].reshape(RATIO * ROWS, HD)
                given = rows_in[pl.ds(spots[h], 1)].reshape(8, RATIO * ROWS)
                ms[h][...] = jnp.broadcast_to(given[:1], (HD, RATIO * ROWS)).T
                ls[h][...] = jnp.broadcast_to(given[1:2] / HD, (HD, RATIO * ROWS)).T

        def quick_step(c, carry):
            near = (c < x) | functools.reduce(jnp.logical_and, [src < z for src in sources])
            whole = near & ((c * XROWS >= first) | (row0 + ROWS <= first))

            @pl.when(whole)
            def _():
                quick(c, False)

            @pl.when(jnp.logical_not(whole))
            def _():
                quick(c, True)

            return carry

        def careful_step(c, carry):
            careful(c, True)
            return carry

        end = x if start else x + 1
        begin()
        lax.fori_loop(low, end, quick_step, 0)

        @pl.when(jnp.logical_not(jnp.max(l_ref[...]) < SAFE))
        def _():
            begin()
            lax.fori_loop(low, end, careful_step, 0)

        for h in range(HEADS):
            if last:
                total = jnp.sum(ls[h][...], axis=-1, keepdims=True)
                o = (accs[h][...] / total).astype(jnp.bfloat16)
                for a, rs in enumerate(heads):
                    out_ref[pl.ds(x, 1), :, at[h * RATIO + a]] = o[rs][None]
            else:
                top = ms[h][...].T[:1]
                total = jnp.sum(ls[h][...].T, axis=0, keepdims=True)
                line = lax.broadcasted_iota(jnp.int32, (8, RATIO * ROWS), 0)
                rows_out[pl.ds(spots[h], 1)] = jnp.where(line == 0, top, total)[None]
        return carry

    lax.fori_loop(0, NX, block, 0)


def stage(ints, q, offsets, shards, ends=(), state=()):
    start, last = not state, bool(ends)
    rows = RATIO * ROWS

    def whole(array):
        return pl.BlockSpec(array.shape, lambda i, s: (0,) * len(array.shape))

    blocks = HEADS * NX
    held = [
        jax.ShapeDtypeStruct((blocks, 8, rows), jnp.float32),
        jax.ShapeDtypeStruct((blocks, rows, HD), jnp.float32),
    ]
    tile = pltpu.VMEM((HEADS, rows, HD), jnp.float32)
    grid = pltpu.PrefetchScalarGridSpec(
        num_scalar_prefetch=1,
        grid=(1,),
        in_specs=[whole(a) for a in (q, *shards, *ends, *state)],
        out_specs=whole(q) if last else [whole(a) for a in held],
        scratch_shapes=[tile] * (3 if last else 2),
    )
    pairs = 7 * HEADS * rows * ROWS * len(offsets)
    return pl.pallas_call(
        functools.partial(stage_kernel, offsets, start, last),
        grid_spec=grid,
        out_shape=jax.ShapeDtypeStruct(q.shape, q.dtype) if last else held,
        compiler_params=pltpu.CompilerParams(vmem_limit_bytes=GRANT),
        cost_estimate=pl.CostEstimate(
            flops=4 * HD * pairs, bytes_accessed=8 << 20, transcendentals=pairs
        ),
        name="prefill_begin" if start else "prefill_end" if last else "prefill_more",
    )(ints, q, *shards, *ends, *state)


def attend(q, parts):
    scores = [jnp.where(ok, nt(q, k), MASKED) for k, _, ok in parts]
    top = functools.reduce(jnp.maximum, [jnp.max(s, axis=-1, keepdims=True) for s in scores])
    total = acc = 0.0
    for s, (_, v, ok) in zip(scores, parts):
        p = jnp.where(ok, jnp.exp2((s - top) * SCALE), 0.0)
        total += jnp.sum(p, axis=-1, keepdims=True)
        acc += nn(p.astype(jnp.bfloat16), v)
    return (acc / total).astype(jnp.bfloat16)


def fresh_ok(rows):
    n = rows * STEPS * RATIO
    row = lax.broadcasted_iota(jnp.int32, (n, rows * STEPS), 0)
    key = lax.broadcasted_iota(jnp.int32, (n, rows * STEPS), 1)
    mine = row // (STEPS * RATIO) == key // STEPS
    return mine & (key % STEPS <= row // RATIO % STEPS)


def cached_kernel(ints, q_ref, kn_ref, vn_ref, k_ref, v_ref, out_ref):
    n = pl.program_id(0)
    slot = ints[I_CTX] * NEW % SLOTS + n
    length = ints[I_LEN + slot]
    q = q_ref[0]
    ok = lax.broadcasted_iota(jnp.int32, (q.shape[0], k_ref.shape[1]), 1) < length
    out_ref[0] = attend(q, [(k_ref[0], v_ref[0], ok), (kn_ref[0], vn_ref[0], fresh_ok(1))])


def decode_cached(ints, q, k_new, v_new, cache_k, cache_v):
    rows, context, _ = cache_k.shape
    n = q.shape[1]

    def whole(shape):
        return pl.BlockSpec((1,) + shape, lambda i, s: (i, 0, 0))

    grid = pltpu.PrefetchScalarGridSpec(
        num_scalar_prefetch=1,
        grid=(rows,),
        in_specs=[
            whole((n, HD)),
            whole((STEPS, HD)),
            whole((STEPS, HD)),
            whole((context, HD)),
            whole((context, HD)),
        ],
        out_specs=whole((n, HD)),
    )
    return pl.pallas_call(
        cached_kernel,
        grid_spec=grid,
        out_shape=jax.ShapeDtypeStruct(q.shape, jnp.bfloat16),
        compiler_params=pltpu.CompilerParams(vmem_limit_bytes=GRANT),
        cost_estimate=pl.CostEstimate(
            flops=4 * HD * rows * context * n,
            bytes_accessed=4 * rows * context * HD,
            transcendentals=rows * context * n,
        ),
        name="decode_cached",
    )(ints, q, k_new, v_new, cache_k, cache_v)


def taken_kernel(offsets, ints, q_ref, kn_ref, vn_ref, *refs):
    *kvs, end_low, end_high, out_ref = refs
    rows = q_ref.shape[0]
    n = rows * STEPS * RATIO
    section = ints[I_SECTION]
    first = ints[I_BLOCKS + 2 * section] * BLOCK
    slot0 = ints[I_CTX] * NEW % SLOTS
    z = ints[I_CTX] % NZ
    q = q_ref[...].reshape(n, HD)
    row = lax.broadcasted_iota(jnp.int32, (n, 1), 0) // (STEPS * RATIO)
    begin = jnp.zeros((n, 1), jnp.int32)
    stop = jnp.zeros((n, 1), jnp.int32)
    for i in range(2):
        mine = row == ints[I_ORDER + SLOTS * section + i] - slot0
        begin = jnp.where(mine, first * i, begin)
        stop = jnp.where(mine, first if i == 0 else NX * XROWS, stop)
    width = NX * ROWS
    col = lax.broadcasted_iota(jnp.int32, (n, width), 1)
    col = col // ROWS * XROWS + col % ROWS
    tail = jnp.concatenate([end_low[...], end_high[...]], axis=0)
    parts = []
    for d, kv in zip(offsets, [kv[...] for kv in kvs] + [tail]):
        token = col + (z + d) % NZ * ROWS
        kv = kv.reshape(width, 2 * HD)
        parts.append((kv[:, :HD], kv[:, HD:], (token >= begin) & (token < stop)))
    kn, vn = [r[...].reshape(rows * STEPS, HD) for r in (kn_ref, vn_ref)]
    out = attend(q, parts + [(kn, vn, fresh_ok(rows))])
    out_ref[...] = out.reshape(out_ref.shape)


def decode_taken(ints, q, k_new, v_new, shards, ends, offsets):
    def one_head(array):
        return pl.BlockSpec(
            (array.shape[0], pl.squeezed, ROWS, 2 * HD),
            lambda i, s: (0, s[I_CTX] % NZ // NEW, 0, 0),
        )

    def whole(array):
        return pl.BlockSpec(array.shape, lambda i, s: (0,) * array.ndim)

    grid = pltpu.PrefetchScalarGridSpec(
        num_scalar_prefetch=1,
        grid=(1,),
        in_specs=[whole(a) for a in (q, k_new, v_new)]
        + [one_head(a) for a in (*shards, *ends)],
        out_specs=whole(q),
    )
    keys = NX * XROWS
    n = q.shape[0] * q.shape[1]
    return pl.pallas_call(
        functools.partial(taken_kernel, offsets),
        grid_spec=grid,
        out_shape=jax.ShapeDtypeStruct(q.shape, jnp.bfloat16),
        compiler_params=pltpu.CompilerParams(vmem_limit_bytes=GRANT),
        cost_estimate=pl.CostEstimate(
            flops=4 * HD * keys * n, bytes_accessed=4 * keys * HD, transcendentals=keys * n
        ),
        name="decode_taken",
    )(ints, q, k_new, v_new, *shards, *ends)


def along_z(value, by):
    pairs = [(x * NZ + z, x * NZ + (z + by) % NZ) for x in range(NX) for z in range(NZ)]
    return lax.ppermute(value, "ctx", pairs)


def per_device(
    q_pf, k_pf, v_pf, pf_blocks, slot_order, cache_k, cache_v, ctx_len, q_dec, k_new, v_new
):
    section = lax.axis_index("section")
    ctx = lax.axis_index("ctx")
    ints = jnp.concatenate(
        [
            jnp.stack([section, ctx]).astype(jnp.int32),
            pf_blocks.reshape(-1),
            slot_order.reshape(-1),
            ctx_len.reshape(-1),
        ]
    )
    swap = [(0, 1), (1, 0)]
    together = lax.optimization_barrier

    def along_x(value):
        return lax.all_to_all(value, "ctx", 0, 0, axis_index_groups=ALONG_X, tiled=True)

    k, v, q = k_pf[0, 0], v_pf[0, 0], q_pf[0, 0]

    def cols(array, head):
        return array[:, head * HD : (head + 1) * HD]

    packed = jnp.stack(
        [
            jnp.concatenate([cols(a, HEADS * x + h) for a in (k, v)], axis=1)
            for x in range(NX)
            for h in range(HEADS)
        ]
    ).reshape(NX, HEADS, ROWS, 2 * HD)
    own_kv = along_x(packed)
    q, own_kv = together((q, own_kv))
    width = HEADS * RATIO * HD
    queries = jnp.stack([q[:, x * width : (x + 1) * width] for x in range(NX)])

    up1, down1 = along_z(own_kv, 1), along_z(own_kv, -1)
    up1, down1, queries, ints = together((up1, down1, queries, ints))
    up2, down2 = along_z(up1, 1), along_z(down1, -1)
    queries = along_x(queries)
    qd, kn, vn = q_dec[0, 0], k_new[0, 0], v_new[0, 0]
    rows = qd.shape[0]
    lists = (rows, STEPS * RATIO, HD)
    own = decode_cached(ints, qd.reshape(lists), kn, vn, cache_k[0, 0], cache_v[0, 0])
    fresh = lax.ppermute(jnp.concatenate([qd, kn, vn], axis=-1), "section", swap)
    up2, down2, own, fresh = together((up2, down2, own, fresh))
    up3, down3 = along_z(up2, 1), along_z(down2, -1)
    near, near_at = [own_kv, up1, down1, up2, down2], [0, -1, 1, -2, 2]
    lines, acc = stage(ints, queries, near_at, near)
    up3, down3, lines = together((up3, down3, lines))
    ends = [along_z(up3[: NX // 2], 1), along_z(down3[NX // 2 :], -1)]
    far, far_at, end_at = [up3, down3], [-3, 3], [4]
    out = stage(ints, queries, far_at + end_at, far, ends, (lines, acc))

    their_q = fresh[..., : RATIO * HD].reshape(lists)
    their_k = fresh[..., RATIO * HD : (RATIO + 1) * HD]
    their_v = fresh[..., (RATIO + 1) * HD :]
    their_q, out = together((their_q, out))
    theirs = decode_taken(
        ints, their_q, their_k, their_v, near + far, ends, near_at + far_at + end_at
    )
    out = along_x(out)
    pf_result = jnp.concatenate([out[x] for x in range(NX)], axis=1)
    back = lax.ppermute(theirs, "section", swap)
    slots = (ctx * rows) % SLOTS + jnp.arange(rows, dtype=jnp.int32)
    taken = slot_order[1 - section, 0, :2]
    is_new = jnp.any(slots[:, None] == taken[None, :], axis=1)
    dec_result = jnp.where(is_new[:, None, None], back, own).reshape(qd.shape)
    return (pf_result[None, None], dec_result[None, None])


def solution(mesh):
    return jax.shard_map(
        per_device,
        mesh=mesh,
        in_specs=(
            P("section", "grp", "ctx", None),
            P("section", "grp", "ctx", None),
            P("section", "grp", "ctx", None),
            P(None, "grp", None),
            P(None, "grp", None),
            P("section", "grp", "ctx", None, None),
            P("section", "grp", "ctx", None, None),
            P("section", "grp", None),
            P("section", "grp", "ctx", None, None),
            P("section", "grp", "ctx", None, None),
            P("section", "grp", "ctx", None, None),
        ),
        out_specs=(P("section", "grp", "ctx", None), P("section", "grp", "ctx", None, None)),
        check_vma=False,
    )
```

```python
import functools
import math

import jax
import jax.numpy as jnp
from jax import lax
from jax.experimental import pallas as pl
from jax.experimental.pallas import tpu as pltpu
from jax.sharding import PartitionSpec as P

HD = 128
BLOCK = 16
NX, NZ = 4, 8
ROWS = 128
XROWS = NZ * ROWS
HEADS = 2
RATIO = 4
STEPS = 4
SLOTS = 16
NEW = 4
MASKED = -1e30
SCALE = math.log2(math.e) / math.sqrt(HD)

ALONG_Z = [[x * NZ + z for z in range(NZ)] for x in range(NX)]
ALONG_X = [[x * NZ + z for x in range(NX)] for z in range(NZ)]

GRANT = 20 << 20

I_SECTION, I_CTX, I_BLOCKS, I_ORDER, I_LEN = 0, 1, 2, 6, 38


def nt(a, b):
    return lax.dot_general(a, b, (((1,), (1,)), ((), ())), preferred_element_type=jnp.float32)


def nn(a, b):
    return lax.dot_general(a, b, (((1,), (0,)), ((), ())), preferred_element_type=jnp.float32)


def move_kernel(plan, *refs):
    *ins, out, sems = refs
    copies = [
        pltpu.make_async_copy(ins[which].at[source], out.at[target], sems.at[i])
        for i, (which, source, target) in enumerate(plan)
    ]
    for copy in copies:
        copy.start()
    for copy in copies:
        copy.wait()


def move(ins, shape, plan, name):
    space = pl.BlockSpec(memory_space=pl.ANY)
    size = 2 * math.prod(shape)
    return pl.pallas_call(
        functools.partial(move_kernel, plan),
        in_specs=[space] * len(ins),
        out_specs=space,
        out_shape=jax.ShapeDtypeStruct(shape, ins[0].dtype),
        scratch_shapes=[pltpu.SemaphoreType.DMA((len(plan),))],
        compiler_params=pltpu.CompilerParams(vmem_limit_bytes=1 << 20),
        cost_estimate=pl.CostEstimate(flops=0, bytes_accessed=2 * size, transcendentals=0),
        name=name,
    )(*ins)


SAFE = 1e30


def stage_kernel(offsets, start, last, ints, q_ref, *refs):
    n = len(offsets)
    z = ints[I_CTX] % NZ
    first = ints[I_BLOCKS + 2 * ints[I_SECTION]] * BLOCK
    sources = [(z + d) % NZ for d in offsets]
    lanes = [slice(g * HD, (g + 1) * HD) for g in range(n)]
    heads = [slice(a * ROWS, (a + 1) * ROWS) for a in range(RATIO)]
    *refs, m_ref, l_ref, worst = refs
    if start:
        *kvs, rows_out, acc_out = refs
    elif not last:
        *kvs, rows_in, acc_in, rows_out, acc_out = refs
    else:
        *kvs, low_half, high_half, rows_in, acc_in, out_ref, acc_end = refs

    def keys_values(h, c):
        both = []
        for part in range(2):

            def one(kv, at):
                return kv[pl.ds(at, 1), part, :, h * HD : (h + 1) * HD].reshape(ROWS, HD)

            blocks = [one(kv, c) for kv in kvs]
            if last:
                half = NX // 2
                pair = [one(kv, c % half) for kv in (low_half, high_half)]
                blocks.append(jnp.where(c < half, *pair))
            both.append(jnp.concatenate(blocks, axis=0))
        return both

    def block(x, quickly):
        row0 = x * XROWS + z * ROWS
        low = jnp.where(row0 >= first, first // XROWS, 0)
        qx = q_ref[pl.ds(x, 1)].reshape(ROWS, HEADS * RATIO * HD)
        at = [slice(a * HD, (a + 1) * HD) for a in range(HEADS * RATIO)]
        qs = [
            jnp.concatenate([qx[:, at[h * RATIO + a]] for a in range(RATIO)], axis=0)
            for h in range(HEADS)
        ]
        spots = [h * NX + x for h in range(HEADS)]
        ms = [m_ref.at[h] for h in range(HEADS)]
        ls = [l_ref.at[h] for h in range(HEADS)]
        accs = [acc_end.at[h] if last else acc_out.at[spots[h]] for h in range(HEADS)]

        def allowed(c):
            row = row0 + lax.broadcasted_iota(jnp.int32, (ROWS, HD), 0)
            lane = c * XROWS + lax.broadcasted_iota(jnp.int32, (ROWS, HD), 1)
            begin = jnp.where(row < first, 0, first)
            return [(lane + src * ROWS <= row) & (lane + src * ROWS >= begin) for src in sources]

        def careful(c, held):
            ok = allowed(c)
            for h in range(HEADS):
                k, v = keys_values(h, c)
                s = nt(qs[h], k)
                ps = []
                for rs in heads:
                    cols = [jnp.where(o, s[rs, g], MASKED) for g, o in zip(lanes, ok)]
                    top = jnp.max(functools.reduce(jnp.maximum, cols), axis=-1, keepdims=True)
                    old = ms[h][rs] if held else None
                    new = jnp.maximum(old, top) if held else jnp.broadcast_to(top, (ROWS, HD))
                    pg = [jnp.exp2((t - new) * SCALE) for t in cols]
                    ms[h][rs] = new
                    total = functools.reduce(jnp.add, pg)
                    if held:
                        fix = jnp.exp2((old - new) * SCALE)
                        ls[h][rs] = ls[h][rs] * fix + total
                        accs[h][rs] = accs[h][rs] * fix
                    else:
                        ls[h][rs] = total
                    ps.append(jnp.concatenate([t.astype(jnp.bfloat16) for t in pg], axis=1))
                o = nn(jnp.concatenate(ps, axis=0), v)
                accs[h][...] = accs[h][...] + o if held else o

        def quick(c, masked):
            ok = allowed(c) if masked else None
            kvh = [keys_values(h, c) for h in range(HEADS)]
            scores = [nt(qs[h], kvh[h][0]) for h in range(HEADS)]
            for h in range(HEADS):
                s = scores[h]
                ps = []
                for rs in heads:
                    m = ms[h][rs]
                    pg = [jnp.exp2((s[rs, g] - m) * SCALE) for g in lanes]
                    if masked:
                        pg = [jnp.where(o, t, 0.0) for o, t in zip(ok, pg)]
                    ls[h][rs] += functools.reduce(jnp.add, pg)
                    ps.append(jnp.concatenate([t.astype(jnp.bfloat16) for t in pg], axis=1))
                accs[h][...] += nn(jnp.concatenate(ps, axis=0), kvh[h][1])

        def begin():
            if start:
                careful(x, False)
                return
            for h in range(HEADS):
                accs[h][...] = acc_in[pl.ds(spots[h], 1)].reshape(RATIO * ROWS, HD)
                given = rows_in[pl.ds(spots[h], 1)].reshape(8, RATIO * ROWS)
                ms[h][...] = jnp.broadcast_to(given[:1], (HD, RATIO * ROWS)).T
                ls[h][...] = jnp.broadcast_to(given[1:2] / HD, (HD, RATIO * ROWS)).T

        def quick_step(c, carry):
            near = (c < x) | functools.reduce(jnp.logical_and, [src < z for src in sources])
            whole = near & ((c * XROWS >= first) | (row0 + ROWS <= first))

            @pl.when(whole)
            def _():
                quick(c, False)

            @pl.when(jnp.logical_not(whole))
            def _():
                quick(c, True)

            return carry

        def careful_step(c, carry):
            careful(c, True)
            return carry

        end = x if start else x + 1
        begin()
        lax.fori_loop(low, end, quick_step if quickly else careful_step, 0)
        if quickly:
            tiles = [ls[h][8 * i : 8 * i + 8] for h in range(HEADS) for i in range(RATIO * ROWS // 8)]
            worst[...] = functools.reduce(jnp.maximum, tiles, worst[...])

        for h in range(HEADS):
            if last:
                total = jnp.sum(ls[h][...], axis=-1, keepdims=True)
                o = (accs[h][...] / total).astype(jnp.bfloat16)
                for a, rs in enumerate(heads):
                    out_ref[pl.ds(x, 1), :, at[h * RATIO + a]] = o[rs][None]
            else:
                top = ms[h][...].T[:1]
                total = jnp.sum(ls[h][...].T, axis=0, keepdims=True)
                line = lax.broadcasted_iota(jnp.int32, (8, RATIO * ROWS), 0)
                rows_out[pl.ds(spots[h], 1)] = jnp.where(line == 0, top, total)[None]

    def blocks(quickly):
        def one(x, carry):
            block(x, quickly)
            return carry

        lax.fori_loop(0, NX, one, 0)

    worst[...] = jnp.zeros(worst.shape, jnp.float32)
    blocks(True)

    @pl.when(jnp.logical_not(jnp.max(worst[...]) < SAFE))
    def _():
        blocks(False)


def stage(ints, q, offsets, shards, ends=(), state=()):
    start, last = not state, bool(ends)
    rows = RATIO * ROWS

    def whole(array):
        return pl.BlockSpec(array.shape, lambda i, s: (0,) * len(array.shape))

    blocks = HEADS * NX
    held = [
        jax.ShapeDtypeStruct((blocks, 8, rows), jnp.float32),
        jax.ShapeDtypeStruct((blocks, rows, HD), jnp.float32),
    ]
    tile = pltpu.VMEM((HEADS, rows, HD), jnp.float32)
    grid = pltpu.PrefetchScalarGridSpec(
        num_scalar_prefetch=1,
        grid=(1,),
        in_specs=[whole(a) for a in (q, *shards, *ends, *state)],
        out_specs=whole(q) if last else [whole(a) for a in held],
        scratch_shapes=[tile] * (3 if last else 2) + [pltpu.VMEM((8, HD), jnp.float32)],
    )
    pairs = 7 * HEADS * rows * ROWS * len(offsets)
    return pl.pallas_call(
        functools.partial(stage_kernel, offsets, start, last),
        grid_spec=grid,
        out_shape=jax.ShapeDtypeStruct(q.shape, q.dtype) if last else held,
        compiler_params=pltpu.CompilerParams(vmem_limit_bytes=GRANT),
        cost_estimate=pl.CostEstimate(
            flops=4 * HD * pairs, bytes_accessed=8 << 20, transcendentals=pairs
        ),
        name="prefill_begin" if start else "prefill_end" if last else "prefill_more",
    )(ints, q, *shards, *ends, *state)


def attend(q, parts):
    scores = [jnp.where(ok, nt(q, k), MASKED) for k, _, ok in parts]
    top = functools.reduce(jnp.maximum, [jnp.max(s, axis=-1, keepdims=True) for s in scores])
    total = acc = 0.0
    for s, (_, v, ok) in zip(scores, parts):
        p = jnp.where(ok, jnp.exp2((s - top) * SCALE), 0.0)
        total += jnp.sum(p, axis=-1, keepdims=True)
        acc += nn(p.astype(jnp.bfloat16), v)
    return (acc / total).astype(jnp.bfloat16)


def fresh_ok(rows):
    n = rows * STEPS * RATIO
    row = lax.broadcasted_iota(jnp.int32, (n, rows * STEPS), 0)
    key = lax.broadcasted_iota(jnp.int32, (n, rows * STEPS), 1)
    mine = row // (STEPS * RATIO) == key // STEPS
    return mine & (key % STEPS <= row // RATIO % STEPS)


def cached_kernel(ints, q_ref, kn_ref, vn_ref, k_ref, v_ref, after_ref, out_ref, keys, values, sems):
    rows = q_ref.shape[0]
    pairs = [(k_ref, keys), (v_ref, values)]
    copies = [
        [pltpu.make_async_copy(src.at[n], dst.at[n], sems.at[i, n]) for i, (src, dst) in enumerate(pairs)]
        for n in range(rows)
    ]
    for pair in copies:
        for copy in pair:
            copy.start()
    slot0 = ints[I_CTX] * NEW % SLOTS
    for n, pair in enumerate(copies):
        q = q_ref[n]
        length = ints[I_LEN + slot0 + n]
        ok = lax.broadcasted_iota(jnp.int32, (q.shape[0], keys.shape[1]), 1) < length
        for copy in pair:
            copy.wait()
        out_ref[n] = attend(q, [(keys[n], values[n], ok), (kn_ref[n], vn_ref[n], fresh_ok(1))])


def decode_cached(ints, q, k_new, v_new, cache_k, cache_v, after):
    rows, context, _ = cache_k.shape
    n = q.shape[1]

    def whole(array):
        return pl.BlockSpec(array.shape, lambda i, s: (0, 0, 0))

    far = pl.BlockSpec(memory_space=pltpu.HBM)
    grid = pltpu.PrefetchScalarGridSpec(
        num_scalar_prefetch=1,
        grid=(1,),
        in_specs=[whole(q), whole(k_new), whole(v_new), far, far, pl.BlockSpec(memory_space=pl.ANY)],
        out_specs=whole(q),
        scratch_shapes=[pltpu.VMEM(cache_k.shape, cache_k.dtype)] * 2
        + [pltpu.SemaphoreType.DMA((2, rows))],
    )
    return pl.pallas_call(
        cached_kernel,
        grid_spec=grid,
        out_shape=jax.ShapeDtypeStruct(q.shape, jnp.bfloat16),
        compiler_params=pltpu.CompilerParams(vmem_limit_bytes=GRANT),
        cost_estimate=pl.CostEstimate(
            flops=4 * HD * rows * context * n,
            bytes_accessed=4 * rows * context * HD,
            transcendentals=rows * context * n,
        ),
        name="decode_cached",
    )(ints, q, k_new, v_new, cache_k, cache_v, after)


def taken_kernel(offsets, ints, q_ref, kn_ref, vn_ref, *refs):
    *kvs, end_low, end_high, out_ref = refs
    rows = q_ref.shape[0]
    n = rows * STEPS * RATIO
    section = ints[I_SECTION]
    first = ints[I_BLOCKS + 2 * section] * BLOCK
    slot0 = ints[I_CTX] * NEW % SLOTS
    z = ints[I_CTX] % NZ
    q = q_ref[...].reshape(n, HD)
    row = lax.broadcasted_iota(jnp.int32, (n, 1), 0) // (STEPS * RATIO)
    begin = jnp.zeros((n, 1), jnp.int32)
    stop = jnp.zeros((n, 1), jnp.int32)
    for i in range(2):
        mine = row == ints[I_ORDER + SLOTS * section + i] - slot0
        begin = jnp.where(mine, first * i, begin)
        stop = jnp.where(mine, first if i == 0 else NX * XROWS, stop)
    width = NX * ROWS
    col = lax.broadcasted_iota(jnp.int32, (n, width), 1)
    col = col // ROWS * XROWS + col % ROWS
    tail = jnp.concatenate([end_low[...], end_high[...]], axis=0)
    parts = []
    for d, kv in zip(offsets, [kv[...] for kv in kvs] + [tail]):
        token = col + (z + d) % NZ * ROWS
        k, v = kv[:, 0].reshape(width, HD), kv[:, 1].reshape(width, HD)
        parts.append((k, v, (token >= begin) & (token < stop)))
    kn, vn = [r[...].reshape(rows * STEPS, HD) for r in (kn_ref, vn_ref)]
    out = attend(q, parts + [(kn, vn, fresh_ok(rows))])
    out_ref[...] = out.reshape(out_ref.shape)


def decode_taken(ints, q, k_new, v_new, shards, ends, offsets):
    def one_head(array):
        return pl.BlockSpec(
            (array.shape[0], 2, ROWS, HD), lambda i, s: (0, 0, 0, s[I_CTX] % NZ // NEW)
        )

    def whole(array):
        return pl.BlockSpec(array.shape, lambda i, s: (0,) * array.ndim)

    grid = pltpu.PrefetchScalarGridSpec(
        num_scalar_prefetch=1,
        grid=(1,),
        in_specs=[whole(a) for a in (q, k_new, v_new)]
        + [one_head(a) for a in (*shards, *ends)],
        out_specs=whole(q),
    )
    keys = NX * XROWS
    n = q.shape[0] * q.shape[1]
    return pl.pallas_call(
        functools.partial(taken_kernel, offsets),
        grid_spec=grid,
        out_shape=jax.ShapeDtypeStruct(q.shape, jnp.bfloat16),
        compiler_params=pltpu.CompilerParams(vmem_limit_bytes=GRANT),
        cost_estimate=pl.CostEstimate(
            flops=4 * HD * keys * n, bytes_accessed=4 * keys * HD, transcendentals=keys * n
        ),
        name="decode_taken",
    )(ints, q, k_new, v_new, *shards, *ends)


def along_z(value, by):
    pairs = [(x * NZ + z, x * NZ + (z + by) % NZ) for x in range(NX) for z in range(NZ)]
    return lax.ppermute(value, "ctx", pairs)


def per_device(
    q_pf, k_pf, v_pf, pf_blocks, slot_order, cache_k, cache_v, ctx_len, q_dec, k_new, v_new
):
    section = lax.axis_index("section")
    ctx = lax.axis_index("ctx")
    ints = jnp.concatenate(
        [
            jnp.stack([section, ctx]).astype(jnp.int32),
            pf_blocks.reshape(-1),
            slot_order.reshape(-1),
            ctx_len.reshape(-1),
        ]
    )
    swap = [(0, 1), (1, 0)]
    together = lax.optimization_barrier

    def along_x(value):
        return lax.all_to_all(value, "ctx", 0, 0, axis_index_groups=ALONG_X, tiled=True)

    k, v, q = k_pf[0, 0], v_pf[0, 0], q_pf[0, 0]

    everything = slice(None)

    def share(x, width):
        return everything, pl.ds(x * width, width)

    kv_width = HEADS * HD
    plan = [(part, share(x, kv_width), (x, part)) for x in range(NX) for part in range(2)]
    packed = move((k, v), (NX, 2, ROWS, kv_width), plan, "pack_kv")
    own_kv = along_x(packed)
    qd, kn, vn = q_dec[0, 0], k_new[0, 0], v_new[0, 0]
    rows = qd.shape[0]
    lists = (rows, STEPS * RATIO, HD)
    own_kv, ints, q = together((own_kv, ints, q))
    width = HEADS * RATIO * HD
    plan = [(0, share(x, width), (x,)) for x in range(NX)]
    queries = along_x(move((q,), (NX, ROWS, width), plan, "pack_q"))

    up1, down1 = along_z(own_kv, 1), along_z(own_kv, -1)
    fresh = lax.ppermute(jnp.concatenate([qd, kn, vn], axis=-1), "section", swap)
    their_q = fresh[..., : RATIO * HD].reshape(lists)
    their_k = fresh[..., RATIO * HD : (RATIO + 1) * HD]
    their_v = fresh[..., (RATIO + 1) * HD :]
    up1, down1, their_q, their_k, their_v = together((up1, down1, their_q, their_k, their_v))
    up2, down2 = along_z(up1, 1), along_z(down1, -1)
    own = decode_cached(ints, qd.reshape(lists), kn, vn, cache_k[0, 0], cache_v[0, 0], up1)
    up2, down2, queries, own = together((up2, down2, queries, own))
    up3, down3 = along_z(up2, 1), along_z(down2, -1)
    near, near_at = [own_kv, up1, down1, up2], [0, -1, 1, -2]
    lines, acc = stage(ints, queries, near_at, near)
    up3, down3, lines = together((up3, down3, lines))
    ends = [along_z(up3[: NX // 2], 1), along_z(down3[NX // 2 :], -1)]
    far, far_at = [down2, up3, down3], [2, -3, 3, 4]
    out = stage(ints, queries, far_at, far, ends, (lines, acc))

    their_q, out = together((their_q, out))
    theirs = decode_taken(
        ints, their_q, their_k, their_v, near + far, ends, near_at + far_at
    )
    out = along_x(out)
    plan = [(0, (x,), share(x, width)) for x in range(NX)]
    pf_result = move((out,), q.shape, plan, "assemble")
    back = lax.ppermute(theirs, "section", swap)
    slots = (ctx * rows) % SLOTS + jnp.arange(rows, dtype=jnp.int32)
    taken = slot_order[1 - section, 0, :2]
    is_new = jnp.any(slots[:, None] == taken[None, :], axis=1)
    dec_result = jnp.where(is_new[:, None, None], back, own).reshape(qd.shape)
    return (pf_result[None, None], dec_result[None, None])


def solution(mesh):
    return jax.shard_map(
        per_device,
        mesh=mesh,
        in_specs=(
            P("section", "grp", "ctx", None),
            P("section", "grp", "ctx", None),
            P("section", "grp", "ctx", None),
            P(None, "grp", None),
            P(None, "grp", None),
            P("section", "grp", "ctx", None, None),
            P("section", "grp", "ctx", None, None),
            P("section", "grp", None),
            P("section", "grp", "ctx", None, None),
            P("section", "grp", "ctx", None, None),
            P("section", "grp", "ctx", None, None),
        ),
        out_specs=(P("section", "grp", "ctx", None), P("section", "grp", "ctx", None, None)),
        check_vma=False,
    )
```

```python
import functools
import math

import jax
import jax.numpy as jnp
from jax import lax
from jax.experimental import pallas as pl
from jax.experimental.pallas import tpu as pltpu
from jax.sharding import PartitionSpec as P

HD = 128
BLOCK = 16
NX, NZ = 4, 8
ROWS = 128
XROWS = NZ * ROWS
HEADS = 2
RATIO = 4
STEPS = 4
SLOTS = 16
NEW = 4
MASKED = -1e30
SCALE = math.log2(math.e) / math.sqrt(HD)

ALONG_Z = [[x * NZ + z for z in range(NZ)] for x in range(NX)]
ALONG_X = [[x * NZ + z for x in range(NX)] for z in range(NZ)]

GRANT = 20 << 20

I_SECTION, I_CTX, I_BLOCKS, I_ORDER, I_LEN = 0, 1, 2, 6, 38


def nt(a, b):
    return lax.dot_general(a, b, (((1,), (1,)), ((), ())), preferred_element_type=jnp.float32)


def nn(a, b):
    return lax.dot_general(a, b, (((1,), (0,)), ((), ())), preferred_element_type=jnp.float32)


def move_kernel(plan, *refs):
    *ins, out, sems = refs
    copies = [
        pltpu.make_async_copy(ins[which].at[source], out.at[target], sems.at[i])
        for i, (which, source, target) in enumerate(plan)
    ]
    for copy in copies:
        copy.start()
    for copy in copies:
        copy.wait()


def move(ins, shape, plan, name):
    space = pl.BlockSpec(memory_space=pl.ANY)
    size = 2 * math.prod(shape)
    return pl.pallas_call(
        functools.partial(move_kernel, plan),
        in_specs=[space] * len(ins),
        out_specs=space,
        out_shape=jax.ShapeDtypeStruct(shape, ins[0].dtype),
        scratch_shapes=[pltpu.SemaphoreType.DMA((len(plan),))],
        compiler_params=pltpu.CompilerParams(vmem_limit_bytes=1 << 20),
        cost_estimate=pl.CostEstimate(flops=0, bytes_accessed=2 * size, transcendentals=0),
        name=name,
    )(*ins)


SAFE = 1e30


def stage_kernel(offsets, start, last, ints, q_ref, *refs):
    n = len(offsets)
    z = ints[I_CTX] % NZ
    first = ints[I_BLOCKS + 2 * ints[I_SECTION]] * BLOCK
    sources = [(z + d) % NZ for d in offsets]
    lanes = [slice(g * HD, (g + 1) * HD) for g in range(n)]
    heads = [slice(a * ROWS, (a + 1) * ROWS) for a in range(RATIO)]
    *refs, m_ref, l_ref, worst = refs
    if start:
        *kvs, rows_out, acc_out = refs
    elif not last:
        *kvs, rows_in, acc_in, rows_out, acc_out = refs
    else:
        *kvs, low_half, high_half, rows_in, acc_in, out_ref, acc_end = refs

    def keys_values(h, c):
        both = []
        for part in range(2):

            def one(kv, at):
                return kv[pl.ds(at, 1), part, :, h * HD : (h + 1) * HD].reshape(ROWS, HD)

            blocks = [one(kv, c) for kv in kvs]
            if last:
                half = NX // 2
                pair = [one(kv, c % half) for kv in (low_half, high_half)]
                blocks.append(jnp.where(c < half, *pair))
            both.append(jnp.concatenate(blocks, axis=0))
        return both

    def block(x, quickly):
        row0 = x * XROWS + z * ROWS
        low = jnp.where(row0 >= first, first // XROWS, 0)
        qx = q_ref[pl.ds(x, 1)].reshape(ROWS, HEADS * RATIO * HD)
        at = [slice(a * HD, (a + 1) * HD) for a in range(HEADS * RATIO)]
        qs = [
            jnp.concatenate([qx[:, at[h * RATIO + a]] for a in range(RATIO)], axis=0)
            for h in range(HEADS)
        ]
        spots = [h * NX + x for h in range(HEADS)]
        ms = [m_ref.at[h] for h in range(HEADS)]
        ls = [l_ref.at[h] for h in range(HEADS)]
        accs = [acc_end.at[h] if last else acc_out.at[spots[h]] for h in range(HEADS)]

        def allowed(c):
            row = row0 + lax.broadcasted_iota(jnp.int32, (ROWS, HD), 0)
            lane = c * XROWS + lax.broadcasted_iota(jnp.int32, (ROWS, HD), 1)
            begin = jnp.where(row < first, 0, first)
            return [(lane + src * ROWS <= row) & (lane + src * ROWS >= begin) for src in sources]

        def careful(c, held):
            ok = allowed(c)
            for h in range(HEADS):
                k, v = keys_values(h, c)
                s = nt(qs[h], k)
                ps = []
                for rs in heads:
                    cols = [jnp.where(o, s[rs, g], MASKED) for g, o in zip(lanes, ok)]
                    top = jnp.max(functools.reduce(jnp.maximum, cols), axis=-1, keepdims=True)
                    old = ms[h][rs] if held else None
                    new = jnp.maximum(old, top) if held else jnp.broadcast_to(top, (ROWS, HD))
                    pg = [jnp.exp2((t - new) * SCALE) for t in cols]
                    ms[h][rs] = new
                    total = functools.reduce(jnp.add, pg)
                    if held:
                        fix = jnp.exp2((old - new) * SCALE)
                        ls[h][rs] = ls[h][rs] * fix + total
                        accs[h][rs] = accs[h][rs] * fix
                    else:
                        ls[h][rs] = total
                    ps.append(jnp.concatenate([t.astype(jnp.bfloat16) for t in pg], axis=1))
                o = nn(jnp.concatenate(ps, axis=0), v)
                accs[h][...] = accs[h][...] + o if held else o

        def quick(c, masked):
            ok = allowed(c) if masked else None
            kvh = [keys_values(h, c) for h in range(HEADS)]
            scores = [nt(qs[h], kvh[h][0]) for h in range(HEADS)]
            for h in range(HEADS):
                s = scores[h]
                ps = []
                for rs in heads:
                    m = ms[h][rs]
                    pg = [jnp.exp2((s[rs, g] - m) * SCALE) for g in lanes]
                    if masked:
                        pg = [jnp.where(o, t, 0.0) for o, t in zip(ok, pg)]
                    ls[h][rs] += functools.reduce(jnp.add, pg)
                    ps.append(jnp.concatenate([t.astype(jnp.bfloat16) for t in pg], axis=1))
                accs[h][...] += nn(jnp.concatenate(ps, axis=0), kvh[h][1])

        def begin():
            if start:
                careful(x, False)
                return
            for h in range(HEADS):
                accs[h][...] = acc_in[pl.ds(spots[h], 1)].reshape(RATIO * ROWS, HD)
                given = rows_in[pl.ds(spots[h], 1)].reshape(8, RATIO * ROWS)
                ms[h][...] = jnp.broadcast_to(given[:1], (HD, RATIO * ROWS)).T
                ls[h][...] = jnp.broadcast_to(given[1:2] / HD, (HD, RATIO * ROWS)).T

        def quick_step(c, carry):
            near = (c < x) | functools.reduce(jnp.logical_and, [src < z for src in sources])
            whole = near & ((c * XROWS >= first) | (row0 + ROWS <= first))

            @pl.when(whole)
            def _():
                quick(c, False)

            @pl.when(jnp.logical_not(whole))
            def _():
                quick(c, True)

            return carry

        def careful_step(c, carry):
            careful(c, True)
            return carry

        end = x if start else x + 1
        begin()
        lax.fori_loop(low, end, quick_step if quickly else careful_step, 0)
        if quickly:
            tiles = [ls[h][8 * i : 8 * i + 8] for h in range(HEADS) for i in range(RATIO * ROWS // 8)]
            worst[...] = functools.reduce(jnp.maximum, tiles, worst[...])

        for h in range(HEADS):
            if last:
                total = jnp.sum(ls[h][...], axis=-1, keepdims=True)
                o = (accs[h][...] / total).astype(jnp.bfloat16)
                for a, rs in enumerate(heads):
                    out_ref[pl.ds(x, 1), :, at[h * RATIO + a]] = o[rs][None]
            else:
                top = ms[h][...].T[:1]
                total = jnp.sum(ls[h][...].T, axis=0, keepdims=True)
                line = lax.broadcasted_iota(jnp.int32, (8, RATIO * ROWS), 0)
                rows_out[pl.ds(spots[h], 1)] = jnp.where(line == 0, top, total)[None]

    def blocks(quickly):
        def one(x, carry):
            block(x, quickly)
            return carry

        lax.fori_loop(0, NX, one, 0)

    worst[...] = jnp.zeros(worst.shape, jnp.float32)
    blocks(True)

    @pl.when(jnp.logical_not(jnp.max(worst[...]) < SAFE))
    def _():
        blocks(False)


def stage(ints, q, offsets, shards, ends=(), state=()):
    start, last = not state, bool(ends)
    rows = RATIO * ROWS

    def whole(array):
        return pl.BlockSpec(array.shape, lambda i, s: (0,) * len(array.shape))

    blocks = HEADS * NX
    held = [
        jax.ShapeDtypeStruct((blocks, 8, rows), jnp.float32),
        jax.ShapeDtypeStruct((blocks, rows, HD), jnp.float32),
    ]
    tile = pltpu.VMEM((HEADS, rows, HD), jnp.float32)
    grid = pltpu.PrefetchScalarGridSpec(
        num_scalar_prefetch=1,
        grid=(1,),
        in_specs=[whole(a) for a in (q, *shards, *ends, *state)],
        out_specs=whole(q) if last else [whole(a) for a in held],
        scratch_shapes=[tile] * (3 if last else 2) + [pltpu.VMEM((8, HD), jnp.float32)],
    )
    pairs = 7 * HEADS * rows * ROWS * len(offsets)
    return pl.pallas_call(
        functools.partial(stage_kernel, offsets, start, last),
        grid_spec=grid,
        out_shape=jax.ShapeDtypeStruct(q.shape, q.dtype) if last else held,
        compiler_params=pltpu.CompilerParams(vmem_limit_bytes=GRANT),
        cost_estimate=pl.CostEstimate(
            flops=4 * HD * pairs, bytes_accessed=8 << 20, transcendentals=pairs
        ),
        name="prefill_begin" if start else "prefill_end" if last else "prefill_more",
    )(ints, q, *shards, *ends, *state)


def attend(q, parts):
    scores = [jnp.where(ok, nt(q, k), MASKED) for k, _, ok in parts]
    top = functools.reduce(jnp.maximum, [jnp.max(s, axis=-1, keepdims=True) for s in scores])
    total = acc = 0.0
    for s, (_, v, ok) in zip(scores, parts):
        p = jnp.where(ok, jnp.exp2((s - top) * SCALE), 0.0)
        total += jnp.sum(p, axis=-1, keepdims=True)
        acc += nn(p.astype(jnp.bfloat16), v)
    return (acc / total).astype(jnp.bfloat16)


def fresh_ok(rows):
    n = rows * STEPS * RATIO
    row = lax.broadcasted_iota(jnp.int32, (n, rows * STEPS), 0)
    key = lax.broadcasted_iota(jnp.int32, (n, rows * STEPS), 1)
    mine = row // (STEPS * RATIO) == key // STEPS
    return mine & (key % STEPS <= row // RATIO % STEPS)


def cached_kernel(ints, q_ref, kn_ref, vn_ref, k_ref, v_ref, after_ref, out_ref, keys, values, sems):
    rows = q_ref.shape[0]
    pairs = [(k_ref, keys), (v_ref, values)]
    copies = [
        [pltpu.make_async_copy(src.at[n], dst.at[n], sems.at[i, n]) for i, (src, dst) in enumerate(pairs)]
        for n in range(rows)
    ]
    for pair in copies:
        for copy in pair:
            copy.start()
    slot0 = ints[I_CTX] * NEW % SLOTS
    for n, pair in enumerate(copies):
        q = q_ref[n]
        length = ints[I_LEN + slot0 + n]
        ok = lax.broadcasted_iota(jnp.int32, (q.shape[0], keys.shape[1]), 1) < length
        for copy in pair:
            copy.wait()
        out_ref[n] = attend(q, [(keys[n], values[n], ok), (kn_ref[n], vn_ref[n], fresh_ok(1))])


def decode_cached(ints, q, k_new, v_new, cache_k, cache_v, after):
    rows, context, _ = cache_k.shape
    n = q.shape[1]

    def whole(array):
        return pl.BlockSpec(array.shape, lambda i, s: (0, 0, 0))

    far = pl.BlockSpec(memory_space=pltpu.HBM)
    grid = pltpu.PrefetchScalarGridSpec(
        num_scalar_prefetch=1,
        grid=(1,),
        in_specs=[whole(q), whole(k_new), whole(v_new), far, far, pl.BlockSpec(memory_space=pl.ANY)],
        out_specs=whole(q),
        scratch_shapes=[pltpu.VMEM(cache_k.shape, cache_k.dtype)] * 2
        + [pltpu.SemaphoreType.DMA((2, rows))],
    )
    return pl.pallas_call(
        cached_kernel,
        grid_spec=grid,
        out_shape=jax.ShapeDtypeStruct(q.shape, jnp.bfloat16),
        compiler_params=pltpu.CompilerParams(vmem_limit_bytes=GRANT),
        cost_estimate=pl.CostEstimate(
            flops=4 * HD * rows * context * n,
            bytes_accessed=4 * rows * context * HD,
            transcendentals=rows * context * n,
        ),
        name="decode_cached",
    )(ints, q, k_new, v_new, cache_k, cache_v, after)


def taken_kernel(offsets, ints, q_ref, kn_ref, vn_ref, *refs):
    *kvs, end_low, end_high, out_ref = refs
    rows = q_ref.shape[0]
    n = rows * STEPS * RATIO
    section = ints[I_SECTION]
    first = ints[I_BLOCKS + 2 * section] * BLOCK
    slot0 = ints[I_CTX] * NEW % SLOTS
    z = ints[I_CTX] % NZ
    q = q_ref[...].reshape(n, HD)
    row = lax.broadcasted_iota(jnp.int32, (n, 1), 0) // (STEPS * RATIO)
    begin = jnp.zeros((n, 1), jnp.int32)
    stop = jnp.zeros((n, 1), jnp.int32)
    for i in range(2):
        mine = row == ints[I_ORDER + SLOTS * section + i] - slot0
        begin = jnp.where(mine, first * i, begin)
        stop = jnp.where(mine, first if i == 0 else NX * XROWS, stop)
    width = NX * ROWS
    col = lax.broadcasted_iota(jnp.int32, (n, width), 1)
    col = col // ROWS * XROWS + col % ROWS
    tail = jnp.concatenate([end_low[...], end_high[...]], axis=0)
    parts = []
    for d, kv in zip(offsets, [kv[...] for kv in kvs] + [tail]):
        token = col + (z + d) % NZ * ROWS
        k, v = kv[:, 0].reshape(width, HD), kv[:, 1].reshape(width, HD)
        parts.append((k, v, (token >= begin) & (token < stop)))
    kn, vn = [r[...].reshape(rows * STEPS, HD) for r in (kn_ref, vn_ref)]
    out = attend(q, parts + [(kn, vn, fresh_ok(rows))])
    out_ref[...] = out.reshape(out_ref.shape)


def decode_taken(ints, q, k_new, v_new, shards, ends, offsets):
    def one_head(array):
        return pl.BlockSpec(
            (array.shape[0], 2, ROWS, HD), lambda i, s: (0, 0, 0, s[I_CTX] % NZ // NEW)
        )

    def whole(array):
        return pl.BlockSpec(array.shape, lambda i, s: (0,) * array.ndim)

    grid = pltpu.PrefetchScalarGridSpec(
        num_scalar_prefetch=1,
        grid=(1,),
        in_specs=[whole(a) for a in (q, k_new, v_new)]
        + [one_head(a) for a in (*shards, *ends)],
        out_specs=whole(q),
    )
    keys = NX * XROWS
    n = q.shape[0] * q.shape[1]
    return pl.pallas_call(
        functools.partial(taken_kernel, offsets),
        grid_spec=grid,
        out_shape=jax.ShapeDtypeStruct(q.shape, jnp.bfloat16),
        compiler_params=pltpu.CompilerParams(vmem_limit_bytes=GRANT),
        cost_estimate=pl.CostEstimate(
            flops=4 * HD * keys * n, bytes_accessed=4 * keys * HD, transcendentals=keys * n
        ),
        name="decode_taken",
    )(ints, q, k_new, v_new, *shards, *ends)


def along_z(value, by):
    pairs = [(x * NZ + z, x * NZ + (z + by) % NZ) for x in range(NX) for z in range(NZ)]
    return lax.ppermute(value, "ctx", pairs)


def per_device(
    q_pf, k_pf, v_pf, pf_blocks, slot_order, cache_k, cache_v, ctx_len, q_dec, k_new, v_new
):
    section = lax.axis_index("section")
    ctx = lax.axis_index("ctx")
    ints = jnp.concatenate(
        [
            jnp.stack([section, ctx]).astype(jnp.int32),
            pf_blocks.reshape(-1),
            slot_order.reshape(-1),
            ctx_len.reshape(-1),
        ]
    )
    swap = [(0, 1), (1, 0)]
    together = lax.optimization_barrier

    def along_x(value):
        return lax.all_to_all(value, "ctx", 0, 0, axis_index_groups=ALONG_X, tiled=True)

    k, v, q = k_pf[0, 0], v_pf[0, 0], q_pf[0, 0]

    everything = slice(None)

    def share(x, width):
        return everything, pl.ds(x * width, width)

    kv_width = HEADS * HD
    plan = [(part, share(x, kv_width), (x, part)) for x in range(NX) for part in range(2)]
    packed = move((k, v), (NX, 2, ROWS, kv_width), plan, "pack_kv")
    own_kv = along_x(packed)
    qd, kn, vn = q_dec[0, 0], k_new[0, 0], v_new[0, 0]
    rows = qd.shape[0]
    lists = (rows, STEPS * RATIO, HD)
    own_kv, ints, q = together((own_kv, ints, q))
    width = HEADS * RATIO * HD
    plan = [(0, share(x, width), (x,)) for x in range(NX)]
    queries = along_x(move((q,), (NX, ROWS, width), plan, "pack_q"))

    up1, down1 = along_z(own_kv, 1), along_z(own_kv, -1)
    fresh = lax.ppermute(jnp.concatenate([qd, kn, vn], axis=-1), "section", swap)
    their_q = fresh[..., : RATIO * HD].reshape(lists)
    their_k = fresh[..., RATIO * HD : (RATIO + 1) * HD]
    their_v = fresh[..., (RATIO + 1) * HD :]
    up1, down1, their_q, their_k, their_v = together((up1, down1, their_q, their_k, their_v))
    up2, down2 = along_z(up1, 1), along_z(down1, -1)
    own = decode_cached(ints, qd.reshape(lists), kn, vn, cache_k[0, 0], cache_v[0, 0], up1)
    down2, queries, own = together((down2, queries, own))
    up3, down3 = along_z(up2, 1), along_z(down2, -1)
    near, near_at = [own_kv, up1, down1, up2], [0, -1, 1, -2]
    lines, acc = stage(ints, queries, near_at, near)
    up3, down3, lines = together((up3, down3, lines))
    ends = [along_z(up3[: NX // 2], 1), along_z(down3[NX // 2 :], -1)]
    far, far_at = [down2, up3, down3], [2, -3, 3, 4]
    out = stage(ints, queries, far_at, far, ends, (lines, acc))

    theirs = decode_taken(
        ints, their_q, their_k, their_v, near + far, ends, near_at + far_at
    )
    out = along_x(out)
    plan = [(0, (x,), share(x, width)) for x in range(NX)]
    pf_result = move((out,), q.shape, plan, "assemble")
    back = lax.ppermute(theirs, "section", swap)
    slots = (ctx * rows) % SLOTS + jnp.arange(rows, dtype=jnp.int32)
    taken = slot_order[1 - section, 0, :2]
    is_new = jnp.any(slots[:, None] == taken[None, :], axis=1)
    dec_result = jnp.where(is_new[:, None, None], back, own).reshape(qd.shape)
    return (pf_result[None, None], dec_result[None, None])


def solution(mesh):
    return jax.shard_map(
        per_device,
        mesh=mesh,
        in_specs=(
            P("section", "grp", "ctx", None),
            P("section", "grp", "ctx", None),
            P("section", "grp", "ctx", None),
            P(None, "grp", None),
            P(None, "grp", None),
            P("section", "grp", "ctx", None, None),
            P("section", "grp", "ctx", None, None),
            P("section", "grp", None),
            P("section", "grp", "ctx", None, None),
            P("section", "grp", "ctx", None, None),
            P("section", "grp", "ctx", None, None),
        ),
        out_specs=(P("section", "grp", "ctx", None), P("section", "grp", "ctx", None, None)),
        check_vma=False,
    )
```
